256 devices in a mesh: dp: 2 (over core), dom: 128 (over y, z, x).
Axes of the slice: x: 4, y: 4, z: 8, core: 2. Of those that a mesh axis runs over, the one named last changes fastest.
Arguments:
- features: bfloat16 [2, 49152, 512], P('dp', 'dom'), may hold values from -12 to 12
- tile_mask: int32 [2, 384, 18], P('dp', 'dom'), may hold values from 0 to 1, as said below
- cotangent: bfloat16 [2, 49152, 512], P('dp', 'dom'), may hold values from -6 to 6
- w_query: bfloat16 [512, 512], replicated, may hold values from -1 to 1
- w_key: bfloat16 [512, 512], replicated, may hold values from -1 to 1
- w_value: bfloat16 [512, 512], replicated, may hold values from -0.25 to 0.25
- w_out: bfloat16 [512, 512], replicated, may hold values from -0.25 to 0.25
Outputs:
- attended: bfloat16 [2, 49152, 512], P('dp', 'dom')
- grad_features: bfloat16 [2, 49152, 512], P('dp', 'dom')
- grad_query: float32 [512, 512], replicated
- grad_key: float32 [512, 512], replicated
- grad_value: float32 [512, 512], replicated
- grad_out: float32 [512, 512], replicated
The draws below stay inside these ranges and needn't reach their ends.
Inputs may be any that keep to these rules, and one draw needn't show every extreme that they name: `tile_mask`: 0 or 1; the share of ones differs between tile groups, from about a quarter to all.
All inputs are finite; a program needn't handle non-finite values.
Results may differ from the reference program's by a relative error of at most 0.023.
Values may be sent and summed in bfloat16 or wider, within the bound.
A program may use at most 128 MiB of HBM per device.

```python
import jax
import jax.numpy as jnp
from jax import lax

HEADS = 8
HEAD_DIM = 64
D = 512
TILE = 128
TILE_DEV = 3
NB = 3
CANDT = 18
QT = 384
NODES = 49152
WINDOWS = 2
N_DOM = 128


def draw_tile_mask(key, part):
    groups = QT // TILE_DEV
    level_key, bit_key = jax.random.split(jax.random.fold_in(key, 11))
    levels = jax.random.randint(level_key, (WINDOWS, groups, 1, 1), 1, 5)
    draws = jax.random.randint(bit_key, (WINDOWS, groups, TILE_DEV, CANDT), 0, 4)
    return (draws < levels).astype(jnp.int32).reshape(WINDOWS, QT, CANDT)


def weight_pair(key):
    primary_key, secondary_key = jax.random.split(jax.random.fold_in(key, 31))
    primary = jnp.clip(jax.random.normal(primary_key, (D, D), jnp.float32), -6.0, 6.0) * D ** (-0.5)
    secondary = jnp.clip(jax.random.normal(secondary_key, (D, D), jnp.float32), -6.0, 6.0) * D ** (-0.5)
    return (primary, secondary)


def draw_w_query(key, part):
    primary, secondary = weight_pair(key)
    return primary.astype(jnp.bfloat16)


def draw_w_key(key, part):
    primary, secondary = weight_pair(key)
    return secondary.astype(jnp.bfloat16)


def draw_features(key, part):
    pieces = jax.random.split(jax.random.fold_in(key, 23), 7)
    drawn = jnp.clip(jax.random.normal(pieces[6], (WINDOWS, NODES, D), jnp.float32), -6.0, 6.0)
    return drawn.astype(jnp.bfloat16)


def block_scale(rng, dims, cuts, least, top_value):
    level = 1.0
    for dim, blocks in cuts:
        heights = jax.random.uniform(jax.random.fold_in(jax.random.fold_in(rng, 6), dim), (blocks,), jnp.float32, least / len(cuts), top_value / len(cuts))
        level = level * jnp.repeat(jnp.exp(heights), dims[dim] // blocks).reshape((-1,) + (1,) * (len(dims) - 1 - dim))
    return level


def centred(rng, dims, scale, most, cuts=(), kind=jnp.bfloat16):
    values = scale * jax.random.normal(rng, dims, jnp.float32)
    if cuts:
        values = values * block_scale(rng, dims, cuts, -0.22, 0.18)
    return jnp.clip(values, -most, most).astype(kind)


def setup_inputs(seed: int = 0) -> dict:
    key_list = jax.random.split(jax.random.key(seed), 8)
    return {
        "features": draw_features(jax.random.fold_in(key_list[7], 71), 0),
        "tile_mask": draw_tile_mask(jax.random.fold_in(key_list[7], 71), 0),
        "cotangent": centred(key_list[2], (WINDOWS, NODES, D), 1.0, 6.0, ((0, 2), (1, 128))),
        "w_query": draw_w_query(jax.random.fold_in(key_list[7], 71), 0),
        "w_key": draw_w_key(jax.random.fold_in(key_list[7], 71), 0),
        "w_value": centred(key_list[5], (D, D), D ** -0.5, 0.25),
        "w_out": centred(key_list[6], (D, D), D ** -0.5, 0.25),
    }


def candidates(device):
    levels = N_DOM.bit_length() - 1
    found = [device, (device - 1) % N_DOM, (device + 1) % N_DOM]
    for bit_step in range(NB):
        found.append(jnp.bitwise_xor(device, jnp.int32(2 ** (levels - 1 - bit_step))))
    return found


def live_table(mask_rows):
    own_tile = jnp.arange(CANDT)[None, :] == jnp.arange(TILE_DEV)[:, None]
    return (mask_rows == 1) | own_tile


def attend(q_rows, cand_kv, live_tiles):
    block_rows = q_rows.shape[0]
    key_count = cand_kv.shape[0]
    head_q = q_rows.reshape(block_rows, HEADS, HEAD_DIM).astype(jnp.float32)
    head_k = cand_kv[:, :D].reshape(key_count, HEADS, HEAD_DIM).astype(jnp.float32)
    head_v = cand_kv[:, D:].reshape(key_count, HEADS, HEAD_DIM).astype(jnp.float32)
    scores = jnp.einsum("rhd,chd->hrc", head_q, head_k) * HEAD_DIM ** -0.5
    masking = jnp.where(live_tiles, 0.0, -1e30).astype(jnp.float32)
    scores = scores.reshape(HEADS, TILE_DEV, TILE, CANDT, TILE) + masking[None, :, None, :, None]
    scores = scores.reshape(HEADS, block_rows, key_count)
    row_max = jnp.max(scores, axis=2, keepdims=True)
    exp_vals = jnp.exp(scores - row_max)
    prob_f32 = exp_vals / jnp.sum(exp_vals, axis=2, keepdims=True)
    prob_bf = lax.optimization_barrier(prob_f32.astype(jnp.bfloat16)).astype(jnp.float32)
    out_rows = jnp.einsum("hrc,chd->rhd", prob_bf, head_v).reshape(block_rows, D).astype(jnp.bfloat16)
    return head_q, head_k, head_v, prob_f32, prob_bf, out_rows


def attend_back(head_q, head_k, head_v, prob_f32, prob_bf, out_rows, grad_o):
    block_rows = head_q.shape[0]
    key_count = head_k.shape[0]
    g_heads = grad_o.reshape(block_rows, HEADS, HEAD_DIM).astype(jnp.float32)
    grad_prob = jnp.einsum("rhd,chd->hrc", g_heads, head_v)
    row_delta = jnp.einsum("rhd,rhd->hr", g_heads, out_rows.reshape(block_rows, HEADS, HEAD_DIM).astype(jnp.float32))
    grad_score = (prob_f32 * (grad_prob - row_delta[:, :, None]) * HEAD_DIM ** -0.5).astype(jnp.bfloat16)
    score_f32 = lax.optimization_barrier(grad_score).astype(jnp.float32)
    grad_q = jnp.einsum("hrc,chd->rhd", score_f32, head_k).reshape(block_rows, D)
    grad_k = jnp.einsum("hrc,rhd->chd", score_f32, head_q).reshape(key_count, D)
    grad_v = jnp.einsum("hrc,rhd->chd", prob_bf, g_heads).reshape(key_count, D)
    return grad_q, jnp.concatenate([grad_k, grad_v], 1)


def window(node_rows, mask_rows, cotangent, w_query, w_both, w_out):
    block_rows = TILE_DEV * TILE
    q_all = jnp.dot(node_rows, w_query, preferred_element_type=jnp.float32).astype(jnp.bfloat16)
    kv_all = jnp.dot(node_rows, w_both, preferred_element_type=jnp.float32).astype(jnp.bfloat16)

    def per_device(grad_acc, device):
        row_start = device * block_rows
        q_rows = lax.dynamic_slice_in_dim(q_all, row_start, block_rows, 0)
        sources = candidates(device)
        cand_kv = jnp.concatenate([lax.dynamic_slice_in_dim(kv_all, (source * block_rows).astype(jnp.int32), block_rows, 0) for source in sources], 0)
        live_tiles = live_table(lax.dynamic_slice_in_dim(mask_rows, (device * TILE_DEV).astype(jnp.int32), TILE_DEV, 0))
        head_q, head_k, head_v, prob_f32, prob_bf, out_rows = attend(q_rows, cand_kv, live_tiles)
        y_rows = jnp.dot(out_rows, w_out, preferred_element_type=jnp.float32).astype(jnp.bfloat16)
        cot_rows = lax.dynamic_slice_in_dim(cotangent, row_start, block_rows, 0)
        grad_o = jnp.dot(cot_rows, w_out.T, preferred_element_type=jnp.float32).astype(jnp.bfloat16)
        grad_q, grad_kv = attend_back(head_q, head_k, head_v, prob_f32, prob_bf, out_rows, grad_o)
        for slot_index, source in enumerate(sources):
            src_start = (source * block_rows).astype(jnp.int32)
            current = lax.dynamic_slice_in_dim(grad_acc, src_start, block_rows, 0)
            piece = grad_kv[slot_index * block_rows:(slot_index + 1) * block_rows]
            grad_acc = lax.dynamic_update_slice_in_dim(grad_acc, current + piece, src_start, 0)
        return grad_acc, (y_rows, out_rows, grad_q)

    grad_acc, stacked = lax.scan(per_device, jnp.zeros((NODES, 2 * D), jnp.float32), jnp.arange(N_DOM, dtype=jnp.int32))
    y_all = stacked[0].reshape(NODES, D)
    o_all = stacked[1].reshape(NODES, D)
    grad_q_all = stacked[2].reshape(NODES, D)
    highest = lax.Precision.HIGHEST
    grad_x = jnp.dot(grad_q_all, w_query.T.astype(jnp.float32), precision=highest)
    grad_x = (grad_x + jnp.dot(grad_acc, w_both.T.astype(jnp.float32), precision=highest)).astype(jnp.bfloat16)
    rows_f32 = node_rows.astype(jnp.float32)
    g_query = jnp.dot(rows_f32.T, grad_q_all, precision=highest)
    g_both = jnp.dot(rows_f32.T, grad_acc, precision=highest)
    g_out = jnp.dot(o_all.T, cotangent, preferred_element_type=jnp.float32)
    return y_all, grad_x, g_query, g_both, g_out


def reference(features, tile_mask, cotangent, w_query, w_key, w_value, w_out):
    w_both = jnp.concatenate([w_key, w_value], 1)
    y_list = []
    gx_list = []
    g_query = jnp.zeros((D, D), jnp.float32)
    g_both = jnp.zeros((D, 2 * D), jnp.float32)
    g_out = jnp.zeros((D, D), jnp.float32)
    for window_index in range(WINDOWS):
        y_all, grad_x, gq_part, gb_part, go_part = window(features[window_index], tile_mask[window_index], cotangent[window_index], w_query, w_both, w_out)
        y_list.append(y_all)
        gx_list.append(grad_x)
        g_query = g_query + gq_part
        g_both = g_both + gb_part
        g_out = g_out + go_part
    return (jnp.stack(y_list), jnp.stack(gx_list), g_query, g_both[:, :D], g_both[:, D:], g_out)
```

```python
import functools
import jax
import jax.numpy as jnp
from jax import lax
from jax.experimental import pallas as pl
from jax.experimental.pallas import tpu as pltpu
from jax.sharding import PartitionSpec as P

BF, F32 = jnp.bfloat16, jnp.float32

ROWS = 384
D = 512
CAND = 6
PAIRS = 4
WIDE = 768
LOG2E = 1.4426950408889634


def nn(a, b):
    return lax.dot_general(a, b, (((1,), (0,)), ((), ())), preferred_element_type=F32)


def nt(a, b):
    return lax.dot_general(a, b, (((1,), (1,)), ((), ())), preferred_element_type=F32)


def block_diag(pair):
    zero = jnp.zeros((64, ROWS), pair.dtype)
    top = jnp.concatenate([pair[:64], zero], 1)
    low = jnp.concatenate([zero, pair[64:]], 1)
    return jnp.concatenate([top, low], 0)


def corners(wide):
    return jnp.concatenate([wide[:64, :ROWS], wide[64:, ROWS:]], 0)


def pair_cols(p, width=128):
    return pl.ds(pl.multiple_of(p * width, width), width)


def prepare(r):
    for p in range(PAIRS):
        r.wkv[:, 256 * p : 256 * p + 128] = r.wk[:, 128 * p : 128 * p + 128]
        r.wkv[:, 256 * p + 128 : 256 * p + 256] = r.wv[:, 128 * p : 128 * p + 128]
    q_t = nn(r.x[0], r.wq[...]).astype(BF).T
    q_t = q_t * jnp.asarray(0.125, BF)
    go_t = nt(r.cot[...], r.wo[...]).astype(BF).T
    for p in range(PAIRS):
        r.qbd[p] = block_diag(q_t[128 * p : 128 * p + 128])
        r.gbd[p] = block_diag(go_t[128 * p : 128 * p + 128])
    r.m[...] = jnp.full_like(r.m, -3e38)
    r.l[...] = jnp.zeros_like(r.l)
    r.o[...] = jnp.zeros_like(r.o)


def project(r, j):
    kv = nn(r.x[j], r.wkv[...]).astype(BF)
    r.kv[j] = kv
    r.kvt[j] = kv.T
    r.xt[:, ROWS * j : ROWS * (j + 1)] = r.x[j].T


def forward(r, j):
    def body(p, _):
        k = r.kv[j, :, pl.ds(pl.multiple_of(p * 256, 256), 128)]
        s = nn(k, r.qbd[p])
        old = r.m[p, 7:8]
        new = old
        shifts = []
        for i in range(3):
            c = 3 * j + i
            top = jnp.max(s[128 * i : 128 * i + 128], axis=0, keepdims=True) + r.bias[c : c + 1]
            new = jnp.maximum(new, top)
        total = jnp.zeros_like(new)
        for i in range(3):
            c = 3 * j + i
            ex = jnp.exp(s[128 * i : 128 * i + 128] - (new - r.bias[c : c + 1]))
            total = total + jnp.sum(ex, axis=0, keepdims=True)
            r.e[p, j, 128 * i : 128 * i + 128] = ex.astype(BF)
        alpha = jnp.exp(old - new)
        r.m[p, 7:8] = new
        r.m[p, j : j + 1] = new
        r.l[p, 0:1] = r.l[p, 0:1] * alpha + total
        vt = r.kvt[j, pl.ds(pl.multiple_of(p * 256 + 128, 128), 128), :]
        r.o[p] = r.o[p] * alpha + nn(vt, r.e[p, j])
        return 0

    lax.fori_loop(0, PAIRS, body, 0)


def finish_forward(r):
    def body(p, _):
        inv = 1.0 / r.l[p, 0:1]
        o_wide = (r.o[p] * inv).astype(BF)
        delta = jnp.sum(r.gbd[p].astype(F32) * o_wide.astype(F32), axis=0, keepdims=True)
        r.l[p, 1:2] = inv
        r.l[p, 2:3] = delta
        o_pair = corners(o_wide)
        r.ot[pair_cols(p), :] = o_pair
        return 0

    lax.fori_loop(0, PAIRS, body, 0)
    r.att[...] = nn(r.ot[...].T, r.wo[...]).astype(BF)
    r.gw[3] = nn(r.ot[...], r.cot[...]).astype(r.gw.dtype)


def backward(r, p, j, gq):
    k_cols = pl.ds(pl.multiple_of(p * 256, 256), 128)
    v_cols = pl.ds(pl.multiple_of(p * 256 + 128, 128), 128)
    gp = nn(r.kv[j, :, v_cols], r.gbd[p])
    gs = (gp - r.l[p, 2:3]).astype(BF) * r.e[p, j]
    scale = jnp.exp(r.m[p, j : j + 1] - r.m[p, 7:8]) * r.l[p, 1:2]
    scaled_q = (r.qbd[p].astype(F32) * scale).astype(BF)
    scaled_g = (r.gbd[p].astype(F32) * scale).astype(BF)
    rows = pl.ds(ROWS * j, ROWS)
    r.gkv[rows, k_cols] = nt(gs, scaled_q).astype(BF)
    r.gkv[rows, v_cols] = nt(r.e[p, j], scaled_g).astype(BF)
    return gq + nn(r.kvt[j, k_cols, :], gs) * scale


def backward_pair(r, p):
    gq = jnp.zeros((128, WIDE), F32)
    for j in range(CAND):
        gq = backward(r, p, j, gq)
    gq_t = (corners(gq) * 0.125).astype(BF)
    r.gqt[pair_cols(p), :] = gq_t
    cols = pair_cols(p)
    r.gw[0, :, cols] = nt(r.xt[:, :ROWS], gq_t).astype(r.gw.dtype)
    both = nn(r.xt[...], r.gkv[:, pl.ds(pl.multiple_of(p * 256, 256), 256)])
    r.gw[1, :, cols] = both[:, :128].astype(r.gw.dtype)
    r.gw[2, :, cols] = both[:, 128:].astype(r.gw.dtype)


def give_back(r, j):
    return nt(r.gkv[ROWS * j : ROWS * (j + 1)], r.wkv[...])


class Refs:
    pass


NAMES_IN = ("x", "cot", "bias", "wq", "wk", "wv", "wo")
SCRATCH = dict(
    wkv=((D, 2 * D), BF),
    qbd=((PAIRS, 128, WIDE), BF),
    gbd=((PAIRS, 128, WIDE), BF),
    m=((PAIRS, 8, WIDE), F32),
    l=((PAIRS, 8, WIDE), F32),
    o=((PAIRS, 128, WIDE), F32),
    ot=((D, ROWS), BF),
    gqt=((D, ROWS), BF),
    kv=((CAND, ROWS, 2 * D), BF),
    kvt=((CAND, 2 * D, ROWS), BF),
    xt=((D, CAND * ROWS), BF),
    e=((PAIRS, CAND, ROWS, WIDE), BF),
    gkv=((CAND * ROWS, 2 * D), BF),
)


def attn_kernel(*refs):
    r = Refs()
    outs = ("att", "back", "own", "gw")
    for name, ref in zip(NAMES_IN + outs + tuple(SCRATCH), refs):
        setattr(r, name, ref)
    prepare(r)
    for j in range(CAND):
        project(r, j)
        forward(r, j)
    finish_forward(r)

    def body(p, _):
        backward_pair(r, p)
        return 0

    lax.fori_loop(0, PAIRS, body, 0)
    for j in range(1, CAND):
        r.back[j - 1] = give_back(r, j).astype(BF)
    r.own[...] = give_back(r, 0) + nt(r.gqt[...].T, r.wq[...])


def attention(x_all, cot, bias, wq, wk, wv, wo):
    vmem = pl.BlockSpec(memory_space=pltpu.VMEM)
    return pl.pallas_call(
        attn_kernel,
        out_shape=(
            jax.ShapeDtypeStruct((ROWS, D), BF),
            jax.ShapeDtypeStruct((CAND - 1, ROWS, D), BF),
            jax.ShapeDtypeStruct((ROWS, D), F32),
            jax.ShapeDtypeStruct((4, D, D), F32),
        ),
        in_specs=[vmem] * 7,
        out_specs=(vmem,) * 4,
        scratch_shapes=[pltpu.VMEM(s, d) for s, d in SCRATCH.values()],
        compiler_params=pltpu.CompilerParams(vmem_limit_bytes=60 * 1024 * 1024),
        name="attention",
    )(x_all, cot, bias, wq, wk, wv, wo)


def masking(tile_mask):
    own = jnp.arange(18)[None, :] == jnp.arange(3)[:, None]
    live = (tile_mask == 1) | own
    b = jnp.where(live, 0.0, -1e30).astype(F32).T
    b = jnp.repeat(b, 128, axis=1)
    return jnp.concatenate([b, b], 1)

MESH = pl.DeviceIdType.MESH
RING_X, RING_Y, RING_Z = (1, 4), (32, 4), (4, 8)
ORDER = ((RING_X, RING_Z, RING_Y), (RING_Y, RING_Z, RING_X))


def place(me, ring):
    stride, size = ring
    return lax.rem(me // stride, size)


def peer(me, ring, step):
    stride, size = ring
    at = place(me, ring)
    return me + (lax.rem(at + step, size) - at) * stride


def partners(me):
    return [lax.rem(me + 1, 128), lax.rem(me + 127, 128), me ^ 64, me ^ 32, me ^ 16]


def greet(me):
    barrier = pltpu.get_barrier_semaphore()
    peers = [peer(me, ring, s) for ring in (RING_X, RING_Y, RING_Z) for s in range(1, ring[1])]
    peers += partners(me)[:2]
    for p in peers:
        pl.semaphore_signal(barrier, inc=1, device_id={"dom": p}, device_id_type=MESH)
    other = 1 - lax.axis_index("dp")
    pl.semaphore_signal(barrier, inc=1, device_id={"dp": other}, device_id_type=MESH)
    pl.semaphore_wait(barrier, len(peers) + 1)


class Reduce:
    def __init__(self, r, me, core, chunk, start, width):
        self.r, self.me, self.core, self.chunk = r, me, core, chunk
        self.lanes = pl.ds(start, width)

    def copy(self, src, dst, color, stage, k, target):
        return pltpu.make_async_remote_copy(
            src_ref=src,
            dst_ref=dst,
            send_sem=self.r.send_sem.at[self.chunk, color, stage, k],
            recv_sem=self.r.recv_sem.at[self.chunk, color, stage, k],
            device_id=target,
            device_id_type=MESH,
        )

    def core_copy(self):
        return self.copy(
            self.r.give.at[:, self.lanes], self.r.got.at[:, self.lanes], 0, 5, 0,
            {"dp": 1 - self.core},
        )

    def first_copies(self, color):
        ring = ORDER[color][0]
        made = []
        for s in range(1, ring[1]):
            to = lax.rem(place(self.me, ring) + s, ring[1])
            made.append(self.copy(
                self.r.half.at[pl.ds(512 * color + to * 128, 128), self.lanes],
                self.r.slot1.at[color, s - 1, :, self.lanes], color, 0, s,
                {"dom": peer(self.me, ring, s)},
            ))
        return made

    def second_copies(self, color):
        ring = ORDER[color][1]
        made = []
        for s in range(1, ring[1]):
            to = lax.rem(place(self.me, ring) + s, ring[1])
            made.append(self.copy(
                self.r.part1.at[color, pl.ds(to * 16, 16), self.lanes],
                self.r.slot2.at[color, s - 1, :, self.lanes], color, 1, s,
                {"dom": peer(self.me, ring, s)},
            ))
        return made

    def third_copies(self, color):
        ring = ORDER[color][2]
        at = place(self.me, ring)
        spot = self.r.slot3.at[color, at, :, self.lanes]
        return [
            self.copy(spot, spot, color, 2, s, {"dom": peer(self.me, ring, s)})
            for s in range(1, ring[1])
        ]

    def result(self, color, row, count):
        return self.r.gw.at[2 * color + row // 256, self.core, pl.ds(lax.rem(row, 256), count), self.lanes]

    def fourth_copies(self, color):
        first, second, _ = ORDER[color]
        row = place(self.me, first) * 128 + place(self.me, second) * 16
        spot = self.result(color, row, 16)
        return [
            self.copy(spot, spot, color, 3, s, {"dom": peer(self.me, second, s)})
            for s in range(1, second[1])
        ]

    def fifth_copies(self, color):
        first = ORDER[color][0]
        spot = self.result(color, place(self.me, first) * 128, 128)
        return [
            self.copy(spot, spot, color, 4, s, {"dom": peer(self.me, first, s)})
            for s in range(1, first[1])
        ]

    def last_copy(self, color):
        spot = self.r.gw.at[pl.ds(2 * color, 2), self.core, :, self.lanes]
        return self.copy(spot, spot, color, 5, 1, {"dp": 1 - self.core})

    def step0(self):
        self.core_copy().start()

    def step1(self):
        self.core_copy().wait()
        r, lanes = self.r, self.lanes
        for b in range(8):
            rows = pl.ds(128 * b, 128)
            t = r.own_half[rows, lanes] + r.got[rows, lanes].astype(F32)
            r.own_half[rows, lanes] = t
            r.half[rows, lanes] = t.astype(BF)
            if b == 3:
                for c in self.first_copies(0):
                    c.start()
        for c in self.first_copies(1):
            c.start()

    def step2(self, color):
        r, lanes = self.r, self.lanes
        for c in self.first_copies(color):
            c.wait()
        at = place(self.me, ORDER[color][0])
        t = r.own_half[pl.ds(512 * color + at * 128, 128), lanes]
        for s in range(3):
            t = t + r.slot1[color, s, :, lanes].astype(F32)
        r.sum1[color, :, lanes] = t
        r.part1[color, :, lanes] = t.astype(BF)
        for c in self.second_copies(color):
            c.start()

    def step3(self, color):
        r, lanes = self.r, self.lanes
        for c in self.second_copies(color):
            c.wait()
        t = r.sum1[color, pl.ds(place(self.me, ORDER[color][1]) * 16, 16), lanes]
        for s in range(7):
            t = t + r.slot2[color, s, :, lanes].astype(F32)
        r.slot3[color, place(self.me, ORDER[color][2]), :, lanes] = t.astype(BF)
        for c in self.third_copies(color):
            c.start()

    def step4(self, color):
        r, lanes = self.r, self.lanes
        for c in self.third_copies(color):
            c.wait()
        t = r.slot3[color, 0, :, lanes].astype(F32)
        for s in range(1, 4):
            t = t + r.slot3[color, s, :, lanes].astype(F32)
        first, second, _ = ORDER[color]
        row = place(self.me, first) * 128 + place(self.me, second) * 16
        r.gw[2 * color + row // 256, self.core, pl.ds(lax.rem(row, 256), 16), lanes] = t.astype(BF)
        for c in self.fourth_copies(color):
            c.start()

    def step5(self, color):
        for c in self.fourth_copies(color):
            c.wait()
        for c in self.fifth_copies(color):
            c.start()

    def step6(self, color):
        for c in self.fifth_copies(color):
            c.wait()
        self.last_copy(color).start()

    def step7(self):
        for color in range(2):
            self.last_copy(color).wait()

    def run(self):
        self.step0()
        self.step1()
        for step in (self.step2, self.step3, self.step4, self.step5, self.step6):
            step(0)
            step(1)
        self.step7()


def reduce_scratch(chunks):
    return dict(
        give=pltpu.VMEM((1024, 512), BF),
        got=pltpu.VMEM((1024, 512), BF),
        own_half=pltpu.VMEM((1024, 512), F32),
        half=pltpu.VMEM((1024, 512), BF),
        slot1=pltpu.VMEM((2, 3, 128, 512), BF),
        sum1=pltpu.VMEM((2, 128, 512), F32),
        part1=pltpu.VMEM((2, 128, 512), BF),
        slot2=pltpu.VMEM((2, 7, 16, 512), BF),
        slot3=pltpu.VMEM((2, 4, 16, 512), BF),
        send_sem=pltpu.SemaphoreType.DMA((chunks, 2, 6, 8)),
        recv_sem=pltpu.SemaphoreType.DMA((chunks, 2, 6, 8)),
    )


def tail_kernel(names, *refs):
    r = Refs()
    for name, ref in zip(names, refs):
        setattr(r, name, ref)
    me, core = lax.axis_index("dom"), lax.axis_index("dp")
    greet(me)
    targets = [lax.rem(me + 127, 128), lax.rem(me + 1, 128), me ^ 64, me ^ 32, me ^ 16]
    back = []
    for j in (4, 2, 0, 1, 3):
        c = pltpu.make_async_remote_copy(
            src_ref=r.back.at[j], dst_ref=r.landed.at[j],
            send_sem=r.ret_send.at[j], recv_sem=r.ret_recv.at[j],
            device_id={"dom": targets[j]}, device_id_type=MESH,
        )
        c.start()
        back.append(c)
    for m in range(4):
        r.give[256 * m : 256 * m + 256] = r.part[m, 1 - core].astype(BF)
        r.own_half[256 * m : 256 * m + 256] = r.part[m, core]
    red = Reduce(r, me, core, 0, 0, 512)
    red.run()
    total = r.own[...]
    for c in back:
        c.wait()
    for j in range(5):
        total = total + r.landed[j].astype(F32)
    r.gx[...] = total.astype(BF)


def tail(back, own, part):
    vmem = pl.BlockSpec(memory_space=pltpu.VMEM)
    scratch = dict(
        landed=pltpu.VMEM((5, 384, 512), BF),
        ret_send=pltpu.SemaphoreType.DMA((5,)),
        ret_recv=pltpu.SemaphoreType.DMA((5,)),
        **reduce_scratch(1),
    )
    names = ("back", "own", "part", "gx", "gw") + tuple(scratch)
    return pl.pallas_call(
        functools.partial(tail_kernel, names),
        out_shape=(
            jax.ShapeDtypeStruct((384, 512), BF),
            jax.ShapeDtypeStruct((4, 2, 256, 512), BF),
        ),
        in_specs=[vmem] * 3,
        out_specs=(vmem,) * 2,
        scratch_shapes=list(scratch.values()),
        compiler_params=pltpu.CompilerParams(
            collective_id=1, has_side_effects=True, vmem_limit_bytes=40 * 1024 * 1024
        ),
        name="return_and_reduce",
    )(back, own, part.reshape(4, 2, 256, 512))


def spread_kernel(x_ref, all_ref, local_sem, send_sem, recv_sem):
    me = lax.axis_index("dom")
    targets = [lax.rem(me + 1, 128), lax.rem(me + 127, 128), me ^ 64, me ^ 32, me ^ 16]
    barrier = pltpu.get_barrier_semaphore()
    for t in targets:
        pl.semaphore_signal(barrier, inc=1, device_id={"dom": t}, device_id_type=MESH)
    pl.semaphore_wait(barrier, 5)
    copies = []
    for j in (4, 2, 0, 1, 3):
        c = pltpu.make_async_remote_copy(
            src_ref=x_ref, dst_ref=all_ref.at[j + 1], send_sem=send_sem.at[j], recv_sem=recv_sem.at[j],
            device_id={"dom": targets[j]}, device_id_type=MESH,
        )
        c.start()
        copies.append(c)
    all_ref[0] = x_ref[...]
    for c in copies:
        c.wait()


def spread(x):
    vmem = pl.BlockSpec(memory_space=pltpu.VMEM)
    return pl.pallas_call(
        spread_kernel,
        out_shape=jax.ShapeDtypeStruct((6, 384, 512), BF),
        in_specs=[vmem],
        out_specs=vmem,
        scratch_shapes=[pltpu.SemaphoreType.DMA, pltpu.SemaphoreType.DMA((5,)), pltpu.SemaphoreType.DMA((5,))],
        compiler_params=pltpu.CompilerParams(collective_id=0, has_side_effects=True),
        name="spread_features",
    )(x)
def per_device(features, tile_mask, cotangent, wq, wk, wv, wo):
    xall=spread(features[0])
    att,back,own,gw=attention(xall,cotangent[0],masking(tile_mask[0]),wq,wk,wv,wo)
    gx,gw=tail(back,own,gw)
    gw=gw.reshape(4,512,512).astype(F32)
    return att[None], gx[None], gw[0],gw[1],gw[2],gw[3]
def solution(mesh):
    s=P("dp","dom",None)
    return jax.shard_map(per_device,mesh=mesh,in_specs=(s,s,s,P(),P(),P(),P()),out_specs=(s,s,P(),P(),P(),P()),check_vma=False)
```

```python
import functools
import jax
import jax.numpy as jnp
from jax import lax
from jax.experimental import pallas as pl
from jax.experimental.pallas import tpu as pltpu
from jax.sharding import PartitionSpec as P

BF, F32 = jnp.bfloat16, jnp.float32

ROWS = 384
D = 512
CAND = 6
PAIRS = 4
WIDE = 768
LOG2E = 1.4426950408889634


def nn(a, b):
    return lax.dot_general(a, b, (((1,), (0,)), ((), ())), preferred_element_type=F32)


def nt(a, b):
    return lax.dot_general(a, b, (((1,), (1,)), ((), ())), preferred_element_type=F32)


def block_diag(pair):
    zero = jnp.zeros((64, ROWS), pair.dtype)
    top = jnp.concatenate([pair[:64], zero], 1)
    low = jnp.concatenate([zero, pair[64:]], 1)
    return jnp.concatenate([top, low], 0)


def corners(wide):
    return jnp.concatenate([wide[:64, :ROWS], wide[64:, ROWS:]], 0)


def pair_cols(p, width=128):
    return pl.ds(pl.multiple_of(p * width, width), width)


def load_copies(r):
    made = [(r.x_hbm, r.x.at[0]), (r.cot_hbm, r.cot), (r.wq_hbm, r.wq), (r.wo_hbm, r.wo)]
    for p in range(PAIRS):
        cols = pl.ds(128 * p, 128)
        made.append((r.wk_hbm.at[:, cols], r.wkv.at[:, pl.ds(256 * p, 128)]))
        made.append((r.wv_hbm.at[:, cols], r.wkv.at[:, pl.ds(256 * p + 128, 128)]))
    return [pltpu.make_async_copy(a, b, r.load_sem.at[i]) for i, (a, b) in enumerate(made)]


def prepare(r):
    q_t = nn(r.x[0], r.wq[...]).astype(BF).T
    q_t = q_t * jnp.asarray(0.125, BF)
    go_t = nt(r.cot[...], r.wo[...]).astype(BF).T
    for p in range(PAIRS):
        r.qbd[p] = block_diag(q_t[128 * p : 128 * p + 128])
        r.gbd[p] = block_diag(go_t[128 * p : 128 * p + 128])
    r.m[...] = jnp.full_like(r.m, -3e38)
    r.l[...] = jnp.zeros_like(r.l)
    r.o[...] = jnp.zeros_like(r.o)


def project(r, j):
    kv = nn(r.x[j], r.wkv[...]).astype(BF)
    r.kv[j] = kv
    r.kvt[j] = kv.T
    r.xt[:, ROWS * j : ROWS * (j + 1)] = r.x[j].T


def forward(r, j):
    def body(p, _):
        k = r.kv[j, :, pl.ds(pl.multiple_of(p * 256, 256), 128)]
        s = nn(k, r.qbd[p])
        old = r.m[p, 7:8]
        new = old
        shifts = []
        for i in range(3):
            c = 3 * j + i
            top = jnp.max(s[128 * i : 128 * i + 128], axis=0, keepdims=True) + r.bias[c : c + 1]
            new = jnp.maximum(new, top)
        total = jnp.zeros_like(new)
        for i in range(3):
            c = 3 * j + i
            ex = jnp.exp(s[128 * i : 128 * i + 128] - (new - r.bias[c : c + 1]))
            total = total + jnp.sum(ex, axis=0, keepdims=True)
            r.e[p, j, 128 * i : 128 * i + 128] = ex.astype(BF)
        alpha = jnp.exp(old - new)
        r.m[p, 7:8] = new
        r.m[p, j : j + 1] = new
        r.l[p, 0:1] = r.l[p, 0:1] * alpha + total
        vt = r.kvt[j, pl.ds(pl.multiple_of(p * 256 + 128, 128), 128), :]
        r.o[p] = r.o[p] * alpha + nn(vt, r.e[p, j])
        return 0

    lax.fori_loop(0, PAIRS, body, 0, unroll=True)


def finish_forward(r):
    def body(p, _):
        inv = 1.0 / r.l[p, 0:1]
        o_wide = (r.o[p] * inv).astype(BF)
        delta = jnp.sum(r.gbd[p].astype(F32) * o_wide.astype(F32), axis=0, keepdims=True)
        r.l[p, 1:2] = inv
        r.l[p, 2:3] = delta
        o_pair = corners(o_wide)
        r.ot[pair_cols(p), :] = o_pair
        return 0

    lax.fori_loop(0, PAIRS, body, 0)
    r.att[...] = nn(r.ot[...].T, r.wo[...]).astype(BF)
    put(r, 3, 0, nn(r.ot[...], r.cot[...]))


def put(r, m, start, value):
    cols = pl.ds(start, value.shape[1])
    r.part[m, 0, :, cols] = value[:256]
    r.part[m, 1, :, cols] = value[256:]


def backward(r, p, j, first):
    k_cols = pl.ds(pl.multiple_of(p * 256, 256), 128)
    v_cols = pl.ds(pl.multiple_of(p * 256 + 128, 128), 128)
    gp = nn(r.kv[j, :, v_cols], r.gbd[p])
    gs = (gp - r.l[p, 2:3]).astype(BF) * r.e[p, j]
    scale = jnp.exp(r.m[p, j : j + 1] - r.m[p, 7:8]) * r.l[p, 1:2]
    scaled_q = (r.qbd[p].astype(F32) * scale).astype(BF)
    scaled_g = (r.gbd[p].astype(F32) * scale).astype(BF)
    rows = pl.ds(ROWS * j, ROWS)
    r.gkv[rows, k_cols] = nt(gs, scaled_q).astype(BF)
    r.gkv[rows, v_cols] = nt(r.e[p, j], scaled_g).astype(BF)
    gq = nn(r.kvt[j, k_cols, :], gs) * scale
    r.o[p] = gq if first else r.o[p] + gq


def finish_pair(r, p):
    gq_t = (corners(r.o[p]) * 0.125).astype(BF)
    r.gqt[pair_cols(p), :] = gq_t
    start = p * 128 if isinstance(p, int) else pl.multiple_of(p * 128, 128)
    put(r, 0, start, nt(r.xt[:, :ROWS], gq_t))
    both = nn(r.xt[...], r.gkv[:, pl.ds(pl.multiple_of(p * 256, 256), 256)])
    put(r, 1, start, both[:, :128])
    put(r, 2, start, both[:, 128:])


def give_back(r, j):
    return nt(r.gkv[ROWS * j : ROWS * (j + 1)], r.wkv[...])


class Refs:
    pass


SCRATCH = dict(
    wkv=((D, 2 * D), BF),
    qbd=((PAIRS, 128, WIDE), BF),
    gbd=((PAIRS, 128, WIDE), BF),
    m=((PAIRS, 8, WIDE), F32),
    l=((PAIRS, 8, WIDE), F32),
    o=((PAIRS, 128, WIDE), F32),
    ot=((D, ROWS), BF),
    gqt=((D, ROWS), BF),
    kv=((CAND, ROWS, 2 * D), BF),
    kvt=((CAND, 2 * D, ROWS), BF),
    xt=((D, CAND * ROWS), BF),
    e=((PAIRS, CAND, ROWS, WIDE), BF),
    gkv=((CAND * ROWS, 2 * D), BF),
    x=((CAND, ROWS, D), BF),
    bias=((3 * CAND, WIDE), F32),
    cot=((ROWS, D), BF),
    wq=((D, D), BF),
    wo=((D, D), BF),
    att=((ROWS, D), BF),
    gx=((ROWS, D), BF),
    own=((ROWS, D), F32),
    back=((CAND - 1, ROWS, D), BF),
    landed=((CAND - 1, ROWS, D), BF),
    part=((4, 2, 256, D), F32),
)


def masking(r):
    for c in range(3 * CAND):
        for t in range(3):
            value = jnp.float32(0.0) if c == t else jnp.where(r.mask[t, c] == 1, 0.0, -1e30)
            row = jnp.full((1, 128), value, F32)
            r.bias[c : c + 1, 128 * t : 128 * t + 128] = row
            r.bias[c : c + 1, ROWS + 128 * t : ROWS + 128 * t + 128] = row


MESH = pl.DeviceIdType.MESH
RING_X, RING_Y, RING_Z = (1, 4), (32, 4), (4, 8)
ORDER = ((RING_X, RING_Z, RING_Y), (RING_Y, RING_Z, RING_X))


def place(me, ring):
    stride, size = ring
    return lax.rem(me // stride, size)


def peer(me, ring, step):
    stride, size = ring
    at = place(me, ring)
    return me + (lax.rem(at + step, size) - at) * stride


def partners(me):
    return [lax.rem(me + 1, 128), lax.rem(me + 127, 128), me ^ 64, me ^ 32, me ^ 16]


def greet(me):
    barrier = pltpu.get_barrier_semaphore()
    peers = [peer(me, ring, s) for ring in (RING_X, RING_Y, RING_Z) for s in range(1, ring[1])]
    peers += partners(me)[:2]
    for p in peers:
        pl.semaphore_signal(barrier, inc=1, device_id={"dom": p}, device_id_type=MESH)
    other = 1 - lax.axis_index("dp")
    pl.semaphore_signal(barrier, inc=1, device_id={"dp": other}, device_id_type=MESH)
    pl.semaphore_wait(barrier, len(peers) + 1)


class Reduce:
    def __init__(self, r, me, core, chunk, start, width):
        self.r, self.me, self.core, self.chunk = r, me, core, chunk
        self.lanes = pl.ds(start, width)

    def copy(self, src, dst, color, stage, k, target):
        return pltpu.make_async_remote_copy(
            src_ref=src,
            dst_ref=dst,
            send_sem=self.r.send_sem.at[self.chunk, color, stage, k],
            recv_sem=self.r.recv_sem.at[self.chunk, color, stage, k],
            device_id=target,
            device_id_type=MESH,
        )

    def core_copy(self):
        return self.copy(
            self.r.give.at[:, self.lanes], self.r.got.at[:, self.lanes], 0, 5, 0,
            {"dp": 1 - self.core},
        )

    def first_copies(self, color):
        ring = ORDER[color][0]
        made = []
        for s in range(1, ring[1]):
            to = lax.rem(place(self.me, ring) + s, ring[1])
            made.append(self.copy(
                self.r.half.at[pl.ds(512 * color + to * 128, 128), self.lanes],
                self.r.slot1.at[color, s - 1, :, self.lanes], color, 0, s,
                {"dom": peer(self.me, ring, s)},
            ))
        return made

    def second_copies(self, color):
        ring = ORDER[color][1]
        made = []
        for s in range(1, ring[1]):
            to = lax.rem(place(self.me, ring) + s, ring[1])
            made.append(self.copy(
                self.r.part1.at[color, pl.ds(to * 16, 16), self.lanes],
                self.r.slot2.at[color, s - 1, :, self.lanes], color, 1, s,
                {"dom": peer(self.me, ring, s)},
            ))
        return made

    def third_copies(self, color):
        ring = ORDER[color][2]
        at = place(self.me, ring)
        spot = self.r.slot3.at[color, at, :, self.lanes]
        return [
            self.copy(spot, spot, color, 2, s, {"dom": peer(self.me, ring, s)})
            for s in range(1, ring[1])
        ]

    def result(self, color, row, count):
        return self.r.gw.at[2 * color + row // 256, self.core, pl.ds(lax.rem(row, 256), count), self.lanes]

    def fourth_copies(self, color):
        first, second, _ = ORDER[color]
        row = place(self.me, first) * 128 + place(self.me, second) * 16
        spot = self.result(color, row, 16)
        return [
            self.copy(spot, spot, color, 3, s, {"dom": peer(self.me, second, s)})
            for s in range(1, second[1])
        ]

    def fifth_copies(self, color):
        first = ORDER[color][0]
        spot = self.result(color, place(self.me, first) * 128, 128)
        return [
            self.copy(spot, spot, color, 4, s, {"dom": peer(self.me, first, s)})
            for s in range(1, first[1])
        ]

    def last_copy(self, color):
        spot = self.r.gw.at[pl.ds(2 * color, 2), self.core, :, self.lanes]
        return self.copy(spot, spot, color, 5, 1, {"dp": 1 - self.core})

    def step0(self):
        r, lanes = self.r, self.lanes
        for m in range(4):
            r.give[256 * m : 256 * m + 256, lanes] = r.part[m, 1 - self.core, :, lanes].astype(BF)
        self.core_copy().start()

    def step1(self):
        self.core_copy().wait()
        r, lanes = self.r, self.lanes
        for b in range(8):
            rows = pl.ds(128 * b, 128)
            t = r.part[b // 2, self.core, 128 * (b % 2) : 128 * (b % 2) + 128, lanes]
            t = t + r.got[rows, lanes].astype(F32)
            r.part[b // 2, self.core, 128 * (b % 2) : 128 * (b % 2) + 128, lanes] = t
            r.half[rows, lanes] = t.astype(BF)
            if b == 3:
                for c in self.first_copies(0):
                    c.start()
        for c in self.first_copies(1):
            c.start()

    def step2(self, color):
        r, lanes = self.r, self.lanes
        for c in self.first_copies(color):
            c.wait()
        at = place(self.me, ORDER[color][0])
        t = r.part[2 * color + at // 2, self.core, pl.ds(lax.rem(at, 2) * 128, 128), lanes]
        for s in range(3):
            t = t + r.slot1[color, s, :, lanes].astype(F32)
        r.sum1[color, :, lanes] = t
        r.part1[color, :, lanes] = t.astype(BF)
        for c in self.second_copies(color):
            c.start()

    def step3(self, color):
        r, lanes = self.r, self.lanes
        for c in self.second_copies(color):
            c.wait()
        t = r.sum1[color, pl.ds(place(self.me, ORDER[color][1]) * 16, 16), lanes]
        for s in range(7):
            t = t + r.slot2[color, s, :, lanes].astype(F32)
        r.slot3[color, place(self.me, ORDER[color][2]), :, lanes] = t.astype(BF)
        for c in self.third_copies(color):
            c.start()

    def step4(self, color):
        r, lanes = self.r, self.lanes
        for c in self.third_copies(color):
            c.wait()
        t = r.slot3[color, 0, :, lanes].astype(F32)
        for s in range(1, 4):
            t = t + r.slot3[color, s, :, lanes].astype(F32)
        first, second, _ = ORDER[color]
        row = place(self.me, first) * 128 + place(self.me, second) * 16
        r.gw[2 * color + row // 256, self.core, pl.ds(lax.rem(row, 256), 16), lanes] = t.astype(BF)
        for c in self.fourth_copies(color):
            c.start()

    def step5(self, color):
        for c in self.fourth_copies(color):
            c.wait()
        for c in self.fifth_copies(color):
            c.start()

    def step6(self, color):
        for c in self.fifth_copies(color):
            c.wait()
        self.last_copy(color).start()

    def step7(self):
        for color in range(2):
            self.last_copy(color).wait()

    def steps(self):
        both = [self.step2, self.step3, self.step4, self.step5, self.step6]
        made = [[self.step0], [self.step1]]
        made += [[functools.partial(step, 0), functools.partial(step, 1)] for step in both]
        return made + [[self.step7]]


def reduce_scratch(chunks):
    return dict(
        give=pltpu.VMEM((1024, 512), BF),
        got=pltpu.VMEM((1024, 512), BF),
        half=pltpu.VMEM((1024, 512), BF),
        slot1=pltpu.VMEM((2, 3, 128, 512), BF),
        sum1=pltpu.VMEM((2, 128, 512), F32),
        part1=pltpu.VMEM((2, 128, 512), BF),
        slot2=pltpu.VMEM((2, 7, 16, 512), BF),
        slot3=pltpu.VMEM((2, 4, 16, 512), BF),
        send_sem=pltpu.SemaphoreType.DMA((chunks, 2, 6, 8)),
        recv_sem=pltpu.SemaphoreType.DMA((chunks, 2, 6, 8)),
    )


CHUNKS = ((0, 512),)
ARRIVALS = (4, 1, 2, 3, 5)
SENDS = (5, 3, 1, 2, 4)


def layer_kernel(names, *refs):
    r = Refs()
    for name, ref in zip(names, refs):
        setattr(r, name, ref)
    me, core = lax.axis_index("dom"), lax.axis_index("dp")
    before, after = lax.rem(me + 127, 128), lax.rem(me + 1, 128)
    sources = (me, before, after, me ^ 64, me ^ 32, me ^ 16)
    holders = (me, after, before, me ^ 64, me ^ 32, me ^ 16)
    loads = load_copies(r)
    for c in loads:
        c.start()
    greet(me)
    spread = {
        j: pltpu.make_async_remote_copy(
            src_ref=r.x_hbm, dst_ref=r.x.at[j], send_sem=r.fwd_send.at[j], recv_sem=r.fwd_recv.at[j],
            device_id={"dom": holders[j]}, device_id_type=MESH,
        )
        for j in SENDS
    }
    returns = {
        j: pltpu.make_async_remote_copy(
            src_ref=r.back.at[j - 1], dst_ref=r.landed.at[j - 1],
            send_sem=r.ret_send.at[j], recv_sem=r.ret_recv.at[j],
            device_id={"dom": sources[j]}, device_id_type=MESH,
        )
        for j in SENDS
    }
    for j in ARRIVALS:
        spread[j].start()
    masking(r)
    for c in loads:
        c.wait()
    prepare(r)
    project(r, 0)
    forward(r, 0)
    for j in ARRIVALS:
        spread[j].wait_recv()
        project(r, j)
        forward(r, j)
    finish_forward(r)
    out = pltpu.make_async_copy(r.att, r.att_hbm, r.out_sem.at[0])
    out.start()

    for i, j in enumerate(SENDS + (0,)):

        def body(p, _, i=i, j=j):
            backward(r, p, j, i == 0)
            return 0

        lax.fori_loop(0, PAIRS, body, 0, unroll=2)
        if j:
            r.back[j - 1] = give_back(r, j).astype(BF)
            returns[j].start()

    def finish(p, _):
        finish_pair(r, p)
        return 0

    lax.fori_loop(0, PAIRS, finish, 0)
    chunks = [Reduce(r, me, core, i, *c).steps() for i, c in enumerate(CHUNKS)]
    running = [chunks[0]]

    def advance():
        for left in running:
            if left:
                for step in left.pop(0):
                    step()

    advance()
    running += chunks[1:]
    r.own[...] = give_back(r, 0) + nt(r.gqt[...].T, r.wq[...])
    advance()
    advance()
    total = r.own[...]
    for j in SENDS:
        returns[j].wait()
        total = total + r.landed[j - 1].astype(F32)
    r.gx[...] = total.astype(BF)
    out_x = pltpu.make_async_copy(r.gx, r.gx_hbm, r.out_sem.at[1])
    out_x.start()
    while any(running):
        advance()
    for j in SENDS:
        spread[j].wait_send()
    out.wait()
    out_x.wait()


def layer(x, cot, mask, wq, wk, wv, wo):
    vmem = pl.BlockSpec(memory_space=pltpu.VMEM)
    hbm = pl.BlockSpec(memory_space=pl.ANY)
    scratch = {name: pltpu.VMEM(s, d) for name, (s, d) in SCRATCH.items()}
    scratch.update(reduce_scratch(len(CHUNKS)))
    for name, count in dict(load_sem=12, fwd_send=6, fwd_recv=6, ret_send=6, ret_recv=6, out_sem=2).items():
        scratch[name] = pltpu.SemaphoreType.DMA((count,))
    names = ("x_hbm", "cot_hbm", "mask", "wq_hbm", "wk_hbm", "wv_hbm", "wo_hbm")
    names += ("att_hbm", "gx_hbm", "gw") + tuple(scratch)
    rows = jax.ShapeDtypeStruct((ROWS, D), BF)
    return pl.pallas_call(
        functools.partial(layer_kernel, names),
        out_shape=(rows, rows, jax.ShapeDtypeStruct((4, 2, 256, D), BF)),
        in_specs=[hbm, hbm, pl.BlockSpec(memory_space=pltpu.SMEM), hbm, hbm, hbm, hbm],
        out_specs=(hbm, hbm, vmem),
        scratch_shapes=list(scratch.values()),
        compiler_params=pltpu.CompilerParams(
            collective_id=0, has_side_effects=True, vmem_limit_bytes=58 * 1024 * 1024
        ),
        name="attention_layer",
    )(x, cot, mask, wq, wk, wv, wo)


def per_device(features, tile_mask, cotangent, wq, wk, wv, wo):
    att, gx, gw = layer(features[0], cotangent[0], tile_mask[0], wq, wk, wv, wo)
    gw = gw.reshape(4, D, D).astype(F32)
    return att[None], gx[None], gw[0], gw[1], gw[2], gw[3]


def solution(mesh):
    s = P("dp", "dom", None)
    return jax.shard_map(
        per_device, mesh=mesh, in_specs=(s, s, s, P(), P(), P(), P()),
        out_specs=(s, s, P(), P(), P(), P()), check_vma=False,
    )
```

```python
import functools
import jax
import jax.numpy as jnp
from jax import lax
from jax.experimental import pallas as pl
from jax.experimental.pallas import tpu as pltpu
from jax.sharding import PartitionSpec as P

BF, F32 = jnp.bfloat16, jnp.float32

ROWS = 384
D = 512
CAND = 6
PAIRS = 4
WIDE = 768
LOG2E = 1.4426950408889634


def nn(a, b):
    return lax.dot_general(a, b, (((1,), (0,)), ((), ())), preferred_element_type=F32)


def nt(a, b):
    return lax.dot_general(a, b, (((1,), (1,)), ((), ())), preferred_element_type=F32)


def block_diag(pair):
    zero = jnp.zeros((64, ROWS), pair.dtype)
    top = jnp.concatenate([pair[:64], zero], 1)
    low = jnp.concatenate([zero, pair[64:]], 1)
    return jnp.concatenate([top, low], 0)


def corners(wide):
    return jnp.concatenate([wide[:64, :ROWS], wide[64:, ROWS:]], 0)


def pair_cols(p, width=128):
    return pl.ds(pl.multiple_of(p * width, width), width)


def load_copies(r):
    made = [(r.x_hbm, r.x.at[0]), (r.cot_hbm, r.cot), (r.wq_hbm, r.wq), (r.wo_hbm, r.wo)]
    for p in range(PAIRS):
        cols = pl.ds(128 * p, 128)
        made.append((r.wk_hbm.at[:, cols], r.wkv.at[:, pl.ds(256 * p, 128)]))
        made.append((r.wv_hbm.at[:, cols], r.wkv.at[:, pl.ds(256 * p + 128, 128)]))
    return [pltpu.make_async_copy(a, b, r.load_sem.at[i]) for i, (a, b) in enumerate(made)]


def prepare(r):
    q_t = nn(r.x[0], r.wq[...]).astype(BF).T
    q_t = q_t * jnp.asarray(0.125, BF)
    go_t = nt(r.cot[...], r.wo[...]).astype(BF).T
    for p in range(PAIRS):
        r.qbd[p] = block_diag(q_t[128 * p : 128 * p + 128])
        r.gbd[p] = block_diag(go_t[128 * p : 128 * p + 128])
    r.m[...] = jnp.full_like(r.m, -3e38)
    r.l[...] = jnp.zeros_like(r.l)
    r.o[...] = jnp.zeros_like(r.o)


def project(r, j):
    kv = nn(r.x[j], r.wkv[...]).astype(BF)
    r.kv[j] = kv
    r.kvt[j] = kv.T
    r.xt[:, ROWS * j : ROWS * (j + 1)] = r.x[j].T


def forward(r, j):
    def body(p, _):
        k = r.kv[j, :, pl.ds(pl.multiple_of(p * 256, 256), 128)]
        s = nn(k, r.qbd[p])
        old = r.m[p, 7:8]
        new = old
        shifts = []
        for i in range(3):
            c = 3 * j + i
            top = jnp.max(s[128 * i : 128 * i + 128], axis=0, keepdims=True) + r.bias[c : c + 1]
            new = jnp.maximum(new, top)
        total = jnp.zeros_like(new)
        for i in range(3):
            c = 3 * j + i
            ex = jnp.exp(s[128 * i : 128 * i + 128] - (new - r.bias[c : c + 1]))
            total = total + jnp.sum(ex, axis=0, keepdims=True)
            r.e[p, j, 128 * i : 128 * i + 128] = ex.astype(BF)
        alpha = jnp.exp(old - new)
        r.m[p, 7:8] = new
        r.m[p, j : j + 1] = new
        r.l[p, 0:1] = r.l[p, 0:1] * alpha + total
        vt = r.kvt[j, pl.ds(pl.multiple_of(p * 256 + 128, 128), 128), :]
        r.o[p] = r.o[p] * alpha + nn(vt, r.e[p, j])
        return 0

    lax.fori_loop(0, PAIRS, body, 0, unroll=True)


def finish_forward(r):
    def body(p, _):
        inv = 1.0 / r.l[p, 0:1]
        o_wide = (r.o[p] * inv).astype(BF)
        delta = jnp.sum(r.gbd[p].astype(F32) * o_wide.astype(F32), axis=0, keepdims=True)
        r.l[p, 1:2] = inv
        r.l[p, 2:3] = delta
        o_pair = corners(o_wide)
        r.ot[pair_cols(p), :] = o_pair
        return 0

    lax.fori_loop(0, PAIRS, body, 0)
    r.att[...] = nn(r.ot[...].T, r.wo[...]).astype(BF)
    put(r, 3, 0, nn(r.ot[...], r.cot[...]))


def put(r, m, start, value):
    cols = pl.ds(start, value.shape[1])
    r.part[m, 0, :, cols] = value[:256]
    r.part[m, 1, :, cols] = value[256:]


def backward(r, p, j, first):
    k_cols = pl.ds(pl.multiple_of(p * 256, 256), 128)
    v_cols = pl.ds(pl.multiple_of(p * 256 + 128, 128), 128)
    gp = nn(r.kv[j, :, v_cols], r.gbd[p])
    gs = (gp - r.l[p, 2:3]).astype(BF) * r.e[p, j]
    scale = jnp.exp(r.m[p, j : j + 1] - r.m[p, 7:8]) * r.l[p, 1:2]
    scaled_q = (r.qbd[p].astype(F32) * scale).astype(BF)
    scaled_g = (r.gbd[p].astype(F32) * scale).astype(BF)
    rows = pl.ds(ROWS * j, ROWS)
    r.gkv[rows, k_cols] = nt(gs, scaled_q).astype(BF)
    r.gkv[rows, v_cols] = nt(r.e[p, j], scaled_g).astype(BF)
    gq = nn(r.kvt[j, k_cols, :], gs) * scale
    r.o[p] = gq if first else r.o[p] + gq


def finish_pair(r, p):
    gq_t = (corners(r.o[p]) * 0.125).astype(BF)
    r.gqt[pair_cols(p), :] = gq_t
    start = p * 128 if isinstance(p, int) else pl.multiple_of(p * 128, 128)
    put(r, 0, start, nt(r.xt[:, :ROWS], gq_t))
    both = nn(r.xt[...], r.gkv[:, pl.ds(pl.multiple_of(p * 256, 256), 256)])
    put(r, 1, start, both[:, :128])
    put(r, 2, start, both[:, 128:])


def give_back(r, j):
    return nt(r.gkv[ROWS * j : ROWS * (j + 1)], r.wkv[...])


class Refs:
    pass


SCRATCH = dict(
    wkv=((D, 2 * D), BF),
    qbd=((PAIRS, 128, WIDE), BF),
    gbd=((PAIRS, 128, WIDE), BF),
    m=((PAIRS, 8, WIDE), F32),
    l=((PAIRS, 8, WIDE), F32),
    o=((PAIRS, 128, WIDE), F32),
    ot=((D, ROWS), BF),
    gqt=((D, ROWS), BF),
    kv=((CAND, ROWS, 2 * D), BF),
    kvt=((CAND, 2 * D, ROWS), BF),
    xt=((D, CAND * ROWS), BF),
    e=((PAIRS, CAND, ROWS, WIDE), BF),
    gkv=((CAND * ROWS, 2 * D), BF),
    x=((CAND, ROWS, D), BF),
    bias=((3 * CAND, WIDE), F32),
    cot=((ROWS, D), BF),
    wq=((D, D), BF),
    wo=((D, D), BF),
    att=((ROWS, D), BF),
    gx=((ROWS, D), BF),
    own=((ROWS, D), F32),
    back=((CAND - 1, ROWS, D), BF),
    landed=((CAND - 1, ROWS, D), BF),
    part=((4, 2, 256, D), F32),
)


def masking(r):
    for c in range(3 * CAND):
        for t in range(3):
            value = jnp.float32(0.0) if c == t else jnp.where(r.mask[0, t, c] == 1, 0.0, -1e30)
            row = jnp.full((1, 128), value, F32)
            r.bias[c : c + 1, 128 * t : 128 * t + 128] = row
            r.bias[c : c + 1, ROWS + 128 * t : ROWS + 128 * t + 128] = row


MESH = pl.DeviceIdType.MESH
RING_X, RING_Y, RING_Z = (1, 4), (32, 4), (4, 8)
ORDER = ((RING_X, RING_Z, RING_Y), (RING_Y, RING_Z, RING_X))


def place(me, ring):
    stride, size = ring
    return lax.rem(me // stride, size)


def peer(me, ring, step):
    stride, size = ring
    at = place(me, ring)
    return me + (lax.rem(at + step, size) - at) * stride


def partners(me):
    return [lax.rem(me + 1, 128), lax.rem(me + 127, 128), me ^ 64, me ^ 32, me ^ 16]


def greet(me):
    barrier = pltpu.get_barrier_semaphore()
    peers = [peer(me, ring, s) for ring in (RING_X, RING_Y, RING_Z) for s in range(1, ring[1])]
    peers += partners(me)[:2]
    for p in peers:
        pl.semaphore_signal(barrier, inc=1, device_id={"dom": p}, device_id_type=MESH)
    other = 1 - lax.axis_index("dp")
    pl.semaphore_signal(barrier, inc=1, device_id={"dp": other}, device_id_type=MESH)
    pl.semaphore_wait(barrier, len(peers) + 1)


class Reduce:
    def __init__(self, r, me, core, chunk, start, width):
        self.r, self.me, self.core, self.chunk = r, me, core, chunk
        self.lanes = pl.ds(start, width)

    def copy(self, src, dst, color, stage, k, target):
        return pltpu.make_async_remote_copy(
            src_ref=src,
            dst_ref=dst,
            send_sem=self.r.send_sem.at[self.chunk, color, stage, k],
            recv_sem=self.r.recv_sem.at[self.chunk, color, stage, k],
            device_id=target,
            device_id_type=MESH,
        )

    def core_copy(self):
        return self.copy(
            self.r.give.at[:, self.lanes], self.r.got.at[:, self.lanes], 0, 5, 0,
            {"dp": 1 - self.core},
        )

    def first_copies(self, color):
        ring = ORDER[color][0]
        made = []
        for s in range(1, ring[1]):
            to = lax.rem(place(self.me, ring) + s, ring[1])
            made.append(self.copy(
                self.r.half.at[pl.ds(512 * color + to * 128, 128), self.lanes],
                self.r.slot1.at[color, s - 1, :, self.lanes], color, 0, s,
                {"dom": peer(self.me, ring, s)},
            ))
        return made

    def second_copies(self, color):
        ring = ORDER[color][1]
        made = []
        for s in range(1, ring[1]):
            to = lax.rem(place(self.me, ring) + s, ring[1])
            made.append(self.copy(
                self.r.part1.at[color, pl.ds(to * 16, 16), self.lanes],
                self.r.slot2.at[color, s - 1, :, self.lanes], color, 1, s,
                {"dom": peer(self.me, ring, s)},
            ))
        return made

    def third_copies(self, color):
        ring = ORDER[color][2]
        at = place(self.me, ring)
        spot = self.r.slot3.at[color, at, :, self.lanes]
        return [
            self.copy(spot, spot, color, 2, s, {"dom": peer(self.me, ring, s)})
            for s in range(1, ring[1])
        ]

    def result(self, color, row, count):
        return self.r.gw.at[2 * color + row // 256, self.core, pl.ds(lax.rem(row, 256), count), self.lanes]

    def fourth_copies(self, color):
        first, second, _ = ORDER[color]
        row = place(self.me, first) * 128 + place(self.me, second) * 16
        spot = self.result(color, row, 16)
        return [
            self.copy(spot, spot, color, 3, s, {"dom": peer(self.me, second, s)})
            for s in range(1, second[1])
        ]

    def fifth_copies(self, color):
        first = ORDER[color][0]
        spot = self.result(color, place(self.me, first) * 128, 128)
        return [
            self.copy(spot, spot, color, 4, s, {"dom": peer(self.me, first, s)})
            for s in range(1, first[1])
        ]

    def last_copies(self, color):
        first = ORDER[color][0]
        at = place(self.me, first)
        made = []
        for s in range(first[1]):
            spot = self.result(color, lax.rem(at + first[1] - s, first[1]) * 128, 128)
            made.append(self.copy(spot, spot, color, 5, 1 + s, {"dp": 1 - self.core}))
        return made

    def step0(self):
        r, lanes = self.r, self.lanes
        for m in range(4):
            r.give[256 * m : 256 * m + 256, lanes] = r.part[m, 1 - self.core, :, lanes].astype(BF)
        self.core_copy().start()

    def step1(self):
        self.core_copy().wait()
        r, lanes = self.r, self.lanes
        for b in range(8):
            rows = pl.ds(128 * b, 128)
            t = r.part[b // 2, self.core, 128 * (b % 2) : 128 * (b % 2) + 128, lanes]
            t = t + r.got[rows, lanes].astype(F32)
            r.part[b // 2, self.core, 128 * (b % 2) : 128 * (b % 2) + 128, lanes] = t
            r.half[rows, lanes] = t.astype(BF)
            if b == 3:
                for c in self.first_copies(0):
                    c.start()
        for c in self.first_copies(1):
            c.start()

    def step2(self, color, pieces):
        r, lanes = self.r, self.lanes
        for piece in pieces:
            for c in piece.first_copies(color):
                c.wait()
        at = place(self.me, ORDER[color][0])
        t = r.part[2 * color + at // 2, self.core, pl.ds(lax.rem(at, 2) * 128, 128), lanes]
        for s in range(3):
            t = t + r.slot1[color, s, :, lanes].astype(F32)
        r.sum1[color, :, lanes] = t
        r.part1[color, :, lanes] = t.astype(BF)
        for c in self.second_copies(color):
            c.start()

    def step3(self, color):
        r, lanes = self.r, self.lanes
        for c in self.second_copies(color):
            c.wait()
        t = r.sum1[color, pl.ds(place(self.me, ORDER[color][1]) * 16, 16), lanes]
        for s in range(7):
            t = t + r.slot2[color, s, :, lanes].astype(F32)
        r.slot3[color, place(self.me, ORDER[color][2]), :, lanes] = t.astype(BF)
        for c in self.third_copies(color):
            c.start()

    def step4(self, color):
        r, lanes = self.r, self.lanes
        for c in self.third_copies(color):
            c.wait()
        t = r.slot3[color, 0, :, lanes].astype(F32)
        for s in range(1, 4):
            t = t + r.slot3[color, s, :, lanes].astype(F32)
        first, second, _ = ORDER[color]
        row = place(self.me, first) * 128 + place(self.me, second) * 16
        r.gw[2 * color + row // 256, self.core, pl.ds(lax.rem(row, 256), 16), lanes] = t.astype(BF)
        for c in self.fourth_copies(color):
            c.start()

    def step5(self, color):
        for c in self.fourth_copies(color):
            c.wait()
        for c in self.fifth_copies(color):
            c.start()
        self.last_copies(color)[0].start()

    def step6(self, color):
        for arrived, handed in zip(self.fifth_copies(color), self.last_copies(color)[1:]):
            arrived.wait()
            handed.start()

    def step7(self):
        for color in range(2):
            for c in self.last_copies(color):
                c.wait()


def reduce_scratch(chunks):
    return dict(
        give=pltpu.VMEM((1024, 512), BF),
        got=pltpu.VMEM((1024, 512), BF),
        half=pltpu.VMEM((1024, 512), BF),
        slot1=pltpu.VMEM((2, 3, 128, 512), BF),
        sum1=pltpu.VMEM((2, 128, 512), F32),
        part1=pltpu.VMEM((2, 128, 512), BF),
        slot2=pltpu.VMEM((2, 7, 16, 512), BF),
        slot3=pltpu.VMEM((2, 4, 16, 512), BF),
        send_sem=pltpu.SemaphoreType.DMA((chunks, 2, 6, 8)),
        recv_sem=pltpu.SemaphoreType.DMA((chunks, 2, 6, 8)),
    )


CHUNKS = ((0, 128), (128, 128), (256, 128), (384, 128))
ARRIVALS = (4, 1, 2, 3, 5)
SENDS = (5, 3, 1, 2, 4)


def layer_kernel(names, *refs):
    r = Refs()
    for name, ref in zip(names, refs):
        setattr(r, name, ref)
    me, core = lax.axis_index("dom"), lax.axis_index("dp")
    before, after = lax.rem(me + 127, 128), lax.rem(me + 1, 128)
    sources = (me, before, after, me ^ 64, me ^ 32, me ^ 16)
    holders = (me, after, before, me ^ 64, me ^ 32, me ^ 16)
    loads = load_copies(r)
    for c in loads:
        c.start()
    greet(me)
    spread = {
        j: pltpu.make_async_remote_copy(
            src_ref=r.x_hbm, dst_ref=r.x.at[j], send_sem=r.fwd_send.at[j], recv_sem=r.fwd_recv.at[j],
            device_id={"dom": holders[j]}, device_id_type=MESH,
        )
        for j in SENDS
    }
    returns = {
        j: pltpu.make_async_remote_copy(
            src_ref=r.back.at[j - 1], dst_ref=r.landed.at[j - 1],
            send_sem=r.ret_send.at[j], recv_sem=r.ret_recv.at[j],
            device_id={"dom": sources[j]}, device_id_type=MESH,
        )
        for j in SENDS
    }
    for j in ARRIVALS:
        spread[j].start()
    masking(r)
    for c in loads:
        c.wait()
    prepare(r)
    project(r, 0)
    forward(r, 0)
    for j in ARRIVALS:
        spread[j].wait_recv()
        project(r, j)
        forward(r, j)
    finish_forward(r)
    out = pltpu.make_async_copy(r.att, r.att_hbm, r.out_sem.at[0])
    out.start()

    for i, j in enumerate(SENDS + (0,)):

        def body(p, _, i=i, j=j):
            backward(r, p, j, i == 0)
            return 0

        lax.fori_loop(0, PAIRS, body, 0, unroll=2)
        if j:
            r.back[j - 1] = give_back(r, j).astype(BF)
            returns[j].start()

    pieces = [Reduce(r, me, core, i, *c) for i, c in enumerate(CHUNKS)]
    for p in range(PAIRS):
        finish_pair(r, p)
        pieces[p].step0()
        if p:
            pieces[p - 1].step1()
    r.own[...] = give_back(r, 0) + nt(r.gqt[...].T, r.wq[...])
    pieces[-1].step1()
    whole = Reduce(r, me, core, 0, 0, 512)
    whole.step2(0, pieces)
    whole.step2(1, pieces)
    total = r.own[...]
    for j in SENDS:
        returns[j].wait()
        total = total + r.landed[j - 1].astype(F32)
    r.gx[...] = total.astype(BF)
    out_x = pltpu.make_async_copy(r.gx, r.gx_hbm, r.out_sem.at[1])
    out_x.start()
    for step in (whole.step3, whole.step4, whole.step5, whole.step6):
        step(0)
        step(1)
    whole.step7()
    for j in SENDS:
        spread[j].wait_send()
    out.wait()
    out_x.wait()


def layer(x, cot, mask, wq, wk, wv, wo):
    vmem = pl.BlockSpec(memory_space=pltpu.VMEM)
    hbm = pl.BlockSpec(memory_space=pl.ANY)
    scratch = {name: pltpu.VMEM(s, d) for name, (s, d) in SCRATCH.items()}
    scratch.update(reduce_scratch(len(CHUNKS)))
    for name, count in dict(load_sem=12, fwd_send=6, fwd_recv=6, ret_send=6, ret_recv=6, out_sem=2).items():
        scratch[name] = pltpu.SemaphoreType.DMA((count,))
    names = ("x_hbm", "cot_hbm", "mask", "wq_hbm", "wk_hbm", "wv_hbm", "wo_hbm")
    names += ("att_hbm", "gx_hbm", "gw") + tuple(scratch)
    rows = jax.ShapeDtypeStruct((ROWS, D), BF)
    return pl.pallas_call(
        functools.partial(layer_kernel, names),
        out_shape=(rows, rows, jax.ShapeDtypeStruct((4, 2, 256, D), BF)),
        in_specs=[hbm, hbm, pl.BlockSpec(memory_space=pltpu.SMEM), hbm, hbm, hbm, hbm],
        out_specs=(hbm, hbm, vmem),
        scratch_shapes=list(scratch.values()),
        compiler_params=pltpu.CompilerParams(
            collective_id=0, has_side_effects=True, vmem_limit_bytes=58 * 1024 * 1024
        ),
        name="attention_layer",
    )(x, cot, mask, wq, wk, wv, wo)


def per_device(features, tile_mask, cotangent, wq, wk, wv, wo):
    att, gx, gw = layer(features[0], cotangent[0], tile_mask, wq, wk, wv, wo)
    gw = gw.reshape(4, D, D).astype(F32)
    return att[None], gx[None], gw[0], gw[1], gw[2], gw[3]


def solution(mesh):
    s = P("dp", "dom", None)
    return jax.shard_map(
        per_device, mesh=mesh, in_specs=(s, s, s, P(), P(), P(), P()),
        out_specs=(s, s, P(), P(), P(), P()), check_vma=False,
    )
```

```python
import functools
import jax
import jax.numpy as jnp
from jax import lax
from jax.experimental import pallas as pl
from jax.experimental.pallas import tpu as pltpu
from jax.sharding import PartitionSpec as P

BF, F32 = jnp.bfloat16, jnp.float32

ROWS = 384
D = 512
CAND = 6
PAIRS = 4
WIDE = 768
LOG2E = 1.4426950408889634


def nn(a, b):
    return lax.dot_general(a, b, (((1,), (0,)), ((), ())), preferred_element_type=F32)


def nt(a, b):
    return lax.dot_general(a, b, (((1,), (1,)), ((), ())), preferred_element_type=F32)


def block_diag(pair):
    zero = jnp.zeros((64, ROWS), pair.dtype)
    top = jnp.concatenate([pair[:64], zero], 1)
    low = jnp.concatenate([zero, pair[64:]], 1)
    return jnp.concatenate([top, low], 0)


def corners(wide):
    return jnp.concatenate([wide[:64, :ROWS], wide[64:, ROWS:]], 0)


def pair_cols(p, width=128):
    return pl.ds(pl.multiple_of(p * width, width), width)


def load_copies(r):
    made = [(r.x_hbm, r.x.at[0]), (r.cot_hbm, r.cot), (r.wq_hbm, r.wq), (r.wo_hbm, r.wo)]
    for p in range(PAIRS):
        cols = pl.ds(128 * p, 128)
        made.append((r.wk_hbm.at[:, cols], r.wkv.at[:, pl.ds(256 * p, 128)]))
        made.append((r.wv_hbm.at[:, cols], r.wkv.at[:, pl.ds(256 * p + 128, 128)]))
    return [pltpu.make_async_copy(a, b, r.load_sem.at[i]) for i, (a, b) in enumerate(made)]


def prepare(r):
    q_t = nn(r.x[0], r.wq[...]).astype(BF).T
    q_t = q_t * jnp.asarray(0.125, BF)
    go_t = nt(r.cot[...], r.wo[...]).astype(BF).T
    for p in range(PAIRS):
        r.qbd[p] = block_diag(q_t[128 * p : 128 * p + 128])
        r.gbd[p] = block_diag(go_t[128 * p : 128 * p + 128])
    r.m[...] = jnp.full_like(r.m, -3e38)
    r.l[...] = jnp.zeros_like(r.l)
    r.o[...] = jnp.zeros_like(r.o)


def project(r, j):
    kv = nn(r.x[j], r.wkv[...]).astype(BF)
    r.kv[j] = kv
    r.kvt[j] = kv.T
    r.xt[:, ROWS * j : ROWS * (j + 1)] = r.x[j].T


def forward(r, j):
    def body(p, _):
        k = r.kv[j, :, pl.ds(pl.multiple_of(p * 256, 256), 128)]
        s = nn(k, r.qbd[p])
        old = r.m[p, 7:8]
        new = old
        shifts = []
        for i in range(3):
            c = 3 * j + i
            top = jnp.max(s[128 * i : 128 * i + 128], axis=0, keepdims=True) + r.bias[c : c + 1]
            new = jnp.maximum(new, top)
        total = jnp.zeros_like(new)
        for i in range(3):
            c = 3 * j + i
            ex = jnp.exp(s[128 * i : 128 * i + 128] - (new - r.bias[c : c + 1]))
            total = total + jnp.sum(ex, axis=0, keepdims=True)
            r.e[p, j, 128 * i : 128 * i + 128] = ex.astype(BF)
        alpha = jnp.exp(old - new)
        r.m[p, 7:8] = new
        r.m[p, j : j + 1] = new
        r.l[p, 0:1] = r.l[p, 0:1] * alpha + total
        vt = r.kvt[j, pl.ds(pl.multiple_of(p * 256 + 128, 128), 128), :]
        r.o[p] = r.o[p] * alpha + nn(vt, r.e[p, j])
        return 0

    lax.fori_loop(0, PAIRS, body, 0, unroll=True)


def finish_forward(r):
    def body(p, _):
        inv = 1.0 / r.l[p, 0:1]
        o_wide = (r.o[p] * inv).astype(BF)
        delta = jnp.sum(r.gbd[p].astype(F32) * o_wide.astype(F32), axis=0, keepdims=True)
        r.l[p, 1:2] = inv
        r.l[p, 2:3] = delta
        o_pair = corners(o_wide)
        r.ot[pair_cols(p), :] = o_pair
        return 0

    lax.fori_loop(0, PAIRS, body, 0)
    r.att[...] = nn(r.ot[...].T, r.wo[...]).astype(BF)
    put(r, 3, 0, nn(r.ot[...], r.cot[...]))


def put(r, m, start, value):
    cols = pl.ds(start, value.shape[1])
    r.part[m, 0, :, cols] = value[:256]
    r.part[m, 1, :, cols] = value[256:]


def backward(r, p, j, first):
    k_cols = pl.ds(pl.multiple_of(p * 256, 256), 128)
    v_cols = pl.ds(pl.multiple_of(p * 256 + 128, 128), 128)
    gp = nn(r.kv[j, :, v_cols], r.gbd[p])
    gs = (gp - r.l[p, 2:3]).astype(BF) * r.e[p, j]
    scale = jnp.exp(r.m[p, j : j + 1] - r.m[p, 7:8]) * r.l[p, 1:2]
    scaled_q = (r.qbd[p].astype(F32) * scale).astype(BF)
    scaled_g = (r.gbd[p].astype(F32) * scale).astype(BF)
    rows = pl.ds(ROWS * j, ROWS)
    r.gkv[rows, k_cols] = nt(gs, scaled_q).astype(BF)
    r.gkv[rows, v_cols] = nt(r.e[p, j], scaled_g).astype(BF)
    gq = nn(r.kvt[j, k_cols, :], gs) * scale
    r.o[p] = gq if first else r.o[p] + gq


def finish_pair(r, p):
    gq_t = (corners(r.o[p]) * 0.125).astype(BF)
    r.gqt[pair_cols(p), :] = gq_t
    start = p * 128 if isinstance(p, int) else pl.multiple_of(p * 128, 128)
    put(r, 0, start, nt(r.xt[:, :ROWS], gq_t))
    both = nn(r.xt[...], r.gkv[:, pl.ds(pl.multiple_of(p * 256, 256), 256)])
    put(r, 1, start, both[:, :128])
    put(r, 2, start, both[:, 128:])


def give_back(r, j):
    return nt(r.gkv[ROWS * j : ROWS * (j + 1)], r.wkv[...])


class Refs:
    pass


SCRATCH = dict(
    wkv=((D, 2 * D), BF),
    qbd=((PAIRS, 128, WIDE), BF),
    gbd=((PAIRS, 128, WIDE), BF),
    m=((PAIRS, 8, WIDE), F32),
    l=((PAIRS, 8, WIDE), F32),
    o=((PAIRS, 128, WIDE), F32),
    ot=((D, ROWS), BF),
    gqt=((D, ROWS), BF),
    kv=((CAND, ROWS, 2 * D), BF),
    kvt=((CAND, 2 * D, ROWS), BF),
    xt=((D, CAND * ROWS), BF),
    e=((PAIRS, CAND, ROWS, WIDE), BF),
    gkv=((CAND * ROWS, 2 * D), BF),
    x=((CAND, ROWS, D), BF),
    bias=((3 * CAND, WIDE), F32),
    cot=((ROWS, D), BF),
    wq=((D, D), BF),
    wo=((D, D), BF),
    att=((ROWS, D), BF),
    gx=((ROWS, D), BF),
    own=((ROWS, D), F32),
    back=((CAND - 1, ROWS, D), BF),
    landed=((CAND - 1, ROWS, D), BF),
    part=((4, 2, 256, D), F32),
)


def masking(r):
    for c in range(3 * CAND):
        for t in range(3):
            value = jnp.float32(0.0) if c == t else jnp.where(r.mask[0, t, c] == 1, 0.0, -1e30)
            row = jnp.full((1, 128), value, F32)
            r.bias[c : c + 1, 128 * t : 128 * t + 128] = row
            r.bias[c : c + 1, ROWS + 128 * t : ROWS + 128 * t + 128] = row


MESH = pl.DeviceIdType.MESH
RING_X, RING_Y, RING_Z = (1, 4), (32, 4), (4, 8)
ORDER = ((RING_X, RING_Z, RING_Y), (RING_Y, RING_Z, RING_X))


def place(me, ring):
    stride, size = ring
    return lax.rem(me // stride, size)


def peer(me, ring, step):
    stride, size = ring
    at = place(me, ring)
    return me + (lax.rem(at + step, size) - at) * stride


def partners(me):
    return [lax.rem(me + 1, 128), lax.rem(me + 127, 128), me ^ 64, me ^ 32, me ^ 16]


def greet(me):
    barrier = pltpu.get_barrier_semaphore()
    peers = [peer(me, ring, s) for ring in (RING_X, RING_Y, RING_Z) for s in range(1, ring[1])]
    peers += partners(me)[:2]
    for p in peers:
        pl.semaphore_signal(barrier, inc=1, device_id={"dom": p}, device_id_type=MESH)
    other = 1 - lax.axis_index("dp")
    pl.semaphore_signal(barrier, inc=1, device_id={"dp": other}, device_id_type=MESH)
    pl.semaphore_wait(barrier, len(peers) + 1)


class Reduce:
    def __init__(self, r, me, core, chunk, start, width):
        self.r, self.me, self.core, self.chunk = r, me, core, chunk
        self.lanes = pl.ds(start, width)

    def copy(self, src, dst, color, stage, k, target):
        return pltpu.make_async_remote_copy(
            src_ref=src,
            dst_ref=dst,
            send_sem=self.r.send_sem.at[self.chunk, color, stage, k],
            recv_sem=self.r.recv_sem.at[self.chunk, color, stage, k],
            device_id=target,
            device_id_type=MESH,
        )

    def core_copy(self):
        return self.copy(
            self.r.give.at[:, self.lanes], self.r.got.at[:, self.lanes], 0, 5, 0,
            {"dp": 1 - self.core},
        )

    def first_copies(self, color):
        ring = ORDER[color][0]
        made = []
        for s in range(1, ring[1]):
            to = lax.rem(place(self.me, ring) + s, ring[1])
            made.append(self.copy(
                self.r.half.at[pl.ds(512 * color + to * 128, 128), self.lanes],
                self.r.slot1.at[color, s - 1, :, self.lanes], color, 0, s,
                {"dom": peer(self.me, ring, s)},
            ))
        return made

    def second_copies(self, color):
        ring = ORDER[color][1]
        made = []
        for s in range(1, ring[1]):
            to = lax.rem(place(self.me, ring) + s, ring[1])
            made.append(self.copy(
                self.r.part1.at[color, pl.ds(to * 16, 16), self.lanes],
                self.r.slot2.at[color, s - 1, :, self.lanes], color, 1, s,
                {"dom": peer(self.me, ring, s)},
            ))
        return made

    def third_copies(self, color):
        ring = ORDER[color][2]
        at = place(self.me, ring)
        spot = self.r.slot3.at[color, at, :, self.lanes]
        return [
            self.copy(spot, spot, color, 2, s, {"dom": peer(self.me, ring, s)})
            for s in range(1, ring[1])
        ]

    def result(self, color, row, count):
        return self.r.gw.at[2 * color + row // 256, self.core, pl.ds(lax.rem(row, 256), count), self.lanes]

    def fourth_copies(self, color):
        first, second, _ = ORDER[color]
        row = place(self.me, first) * 128 + place(self.me, second) * 16
        spot = self.result(color, row, 16)
        return [
            self.copy(spot, spot, color, 3, s, {"dom": peer(self.me, second, s)})
            for s in range(1, second[1])
        ]

    def fifth_copies(self, color):
        first = ORDER[color][0]
        spot = self.result(color, place(self.me, first) * 128, 128)
        return [
            self.copy(spot, spot, color, 4, s, {"dom": peer(self.me, first, s)})
            for s in range(1, first[1])
        ]

    def last_copies(self, color):
        first = ORDER[color][0]
        at = place(self.me, first)
        made = []
        for s in range(first[1]):
            spot = self.result(color, lax.rem(at + first[1] - s, first[1]) * 128, 128)
            made.append(self.copy(spot, spot, color, 5, 1 + s, {"dp": 1 - self.core}))
        return made

    def step0(self):
        r, lanes = self.r, self.lanes
        for m in range(4):
            r.give[256 * m : 256 * m + 256, lanes] = r.part[m, 1 - self.core, :, lanes].astype(BF)
        self.core_copy().start()

    def step1(self):
        self.core_copy().wait()
        r, lanes = self.r, self.lanes
        for b in range(8):
            rows = pl.ds(128 * b, 128)
            t = r.part[b // 2, self.core, 128 * (b % 2) : 128 * (b % 2) + 128, lanes]
            t = t + r.got[rows, lanes].astype(F32)
            r.part[b // 2, self.core, 128 * (b % 2) : 128 * (b % 2) + 128, lanes] = t
            r.half[rows, lanes] = t.astype(BF)
            if b == 3:
                for c in self.first_copies(0):
                    c.start()
        for c in self.first_copies(1):
            c.start()

    def step2(self, color):
        r, lanes = self.r, self.lanes
        for c in self.first_copies(color):
            c.wait()
        at = place(self.me, ORDER[color][0])
        t = r.part[2 * color + at // 2, self.core, pl.ds(lax.rem(at, 2) * 128, 128), lanes]
        for s in range(3):
            t = t + r.slot1[color, s, :, lanes].astype(F32)
        r.sum1[color, :, lanes] = t
        r.part1[color, :, lanes] = t.astype(BF)
        for c in self.second_copies(color):
            c.start()

    def step3(self, color):
        r, lanes = self.r, self.lanes
        for c in self.second_copies(color):
            c.wait()
        t = r.sum1[color, pl.ds(place(self.me, ORDER[color][1]) * 16, 16), lanes]
        for s in range(7):
            t = t + r.slot2[color, s, :, lanes].astype(F32)
        r.slot3[color, place(self.me, ORDER[color][2]), :, lanes] = t.astype(BF)
        for c in self.third_copies(color):
            c.start()

    def step4(self, color):
        r, lanes = self.r, self.lanes
        for c in self.third_copies(color):
            c.wait()
        t = r.slot3[color, 0, :, lanes].astype(F32)
        for s in range(1, 4):
            t = t + r.slot3[color, s, :, lanes].astype(F32)
        first, second, _ = ORDER[color]
        row = place(self.me, first) * 128 + place(self.me, second) * 16
        r.gw[2 * color + row // 256, self.core, pl.ds(lax.rem(row, 256), 16), lanes] = t.astype(BF)
        for c in self.fourth_copies(color):
            c.start()

    def step5(self, color):
        for c in self.fourth_copies(color):
            c.wait()
        for c in self.fifth_copies(color):
            c.start()
        self.last_copies(color)[0].start()

    def step6(self, color):
        for arrived, handed in zip(self.fifth_copies(color), self.last_copies(color)[1:]):
            arrived.wait()
            handed.start()

    def step7(self):
        for color in range(2):
            for c in self.last_copies(color):
                c.wait()


def reduce_scratch(chunks):
    return dict(
        give=pltpu.VMEM((1024, 512), BF),
        got=pltpu.VMEM((1024, 512), BF),
        half=pltpu.VMEM((1024, 512), BF),
        slot1=pltpu.VMEM((2, 3, 128, 512), BF),
        sum1=pltpu.VMEM((2, 128, 512), F32),
        part1=pltpu.VMEM((2, 128, 512), BF),
        slot2=pltpu.VMEM((2, 7, 16, 512), BF),
        slot3=pltpu.VMEM((2, 4, 16, 512), BF),
        send_sem=pltpu.SemaphoreType.DMA((chunks, 2, 6, 8)),
        recv_sem=pltpu.SemaphoreType.DMA((chunks, 2, 6, 8)),
    )


ARRIVALS = (4, 1, 2, 3, 5)
SENDS = (5, 3, 1, 2, 4)


def layer_kernel(names, *refs):
    r = Refs()
    for name, ref in zip(names, refs):
        setattr(r, name, ref)
    me, core = lax.axis_index("dom"), lax.axis_index("dp")
    before, after = lax.rem(me + 127, 128), lax.rem(me + 1, 128)
    sources = (me, before, after, me ^ 64, me ^ 32, me ^ 16)
    holders = (me, after, before, me ^ 64, me ^ 32, me ^ 16)
    loads = load_copies(r)
    for c in loads:
        c.start()
    greet(me)
    spread = {
        j: pltpu.make_async_remote_copy(
            src_ref=r.x_hbm, dst_ref=r.x.at[j], send_sem=r.fwd_send.at[j], recv_sem=r.fwd_recv.at[j],
            device_id={"dom": holders[j]}, device_id_type=MESH,
        )
        for j in SENDS
    }
    returns = {
        j: pltpu.make_async_remote_copy(
            src_ref=r.back.at[j - 1], dst_ref=r.landed.at[j - 1],
            send_sem=r.ret_send.at[j], recv_sem=r.ret_recv.at[j],
            device_id={"dom": sources[j]}, device_id_type=MESH,
        )
        for j in SENDS
    }
    for j in ARRIVALS:
        spread[j].start()
    masking(r)
    for c in loads:
        c.wait()
    prepare(r)
    project(r, 0)
    forward(r, 0)
    for j in ARRIVALS:
        spread[j].wait_recv()
        project(r, j)
        forward(r, j)
    finish_forward(r)
    out = pltpu.make_async_copy(r.att, r.att_hbm, r.out_sem.at[0])
    out.start()

    for i, j in enumerate(SENDS + (0,)):

        def body(p, _, i=i, j=j):
            backward(r, p, j, i == 0)
            return 0

        lax.fori_loop(0, PAIRS, body, 0, unroll=2)
        if j:
            r.back[j - 1] = give_back(r, j).astype(BF)
            returns[j].start()

    def finish(p, _):
        finish_pair(r, p)
        return 0

    lax.fori_loop(0, PAIRS, finish, 0)
    whole = Reduce(r, me, core, 0, 0, 512)
    whole.step0()
    r.own[...] = give_back(r, 0) + nt(r.gqt[...].T, r.wq[...])
    whole.step1()
    whole.step2(0)
    whole.step2(1)
    total = r.own[...]
    for j in SENDS:
        returns[j].wait()
        total = total + r.landed[j - 1].astype(F32)
    r.gx[...] = total.astype(BF)
    out_x = pltpu.make_async_copy(r.gx, r.gx_hbm, r.out_sem.at[1])
    out_x.start()
    for step in (whole.step3, whole.step4, whole.step5, whole.step6):
        step(0)
        step(1)
    whole.step7()
    for j in SENDS:
        spread[j].wait_send()
    out.wait()
    out_x.wait()


def layer(x, cot, mask, wq, wk, wv, wo):
    vmem = pl.BlockSpec(memory_space=pltpu.VMEM)
    hbm = pl.BlockSpec(memory_space=pl.ANY)
    scratch = {name: pltpu.VMEM(s, d) for name, (s, d) in SCRATCH.items()}
    scratch.update(reduce_scratch(1))
    for name, count in dict(load_sem=12, fwd_send=6, fwd_recv=6, ret_send=6, ret_recv=6, out_sem=2).items():
        scratch[name] = pltpu.SemaphoreType.DMA((count,))
    names = ("x_hbm", "cot_hbm", "mask", "wq_hbm", "wk_hbm", "wv_hbm", "wo_hbm")
    names += ("att_hbm", "gx_hbm", "gw") + tuple(scratch)
    rows = jax.ShapeDtypeStruct((ROWS, D), BF)
    return pl.pallas_call(
        functools.partial(layer_kernel, names),
        out_shape=(rows, rows, jax.ShapeDtypeStruct((4, 2, 256, D), BF)),
        in_specs=[hbm, hbm, pl.BlockSpec(memory_space=pltpu.SMEM), hbm, hbm, hbm, hbm],
        out_specs=(hbm, hbm, vmem),
        scratch_shapes=list(scratch.values()),
        compiler_params=pltpu.CompilerParams(
            collective_id=0, has_side_effects=True, vmem_limit_bytes=58 * 1024 * 1024
        ),
        name="attention_layer",
    )(x, cot, mask, wq, wk, wv, wo)


def per_device(features, tile_mask, cotangent, wq, wk, wv, wo):
    att, gx, gw = layer(features[0], cotangent[0], tile_mask, wq, wk, wv, wo)
    gw = gw.reshape(4, D, D).astype(F32)
    return att[None], gx[None], gw[0], gw[1], gw[2], gw[3]


def solution(mesh):
    s = P("dp", "dom", None)
    return jax.shard_map(
        per_device, mesh=mesh, in_specs=(s, s, s, P(), P(), P(), P()),
        out_specs=(s, s, P(), P(), P(), P()), check_vma=False,
    )
```
